32 devices in a mesh: dp: 16 (over z, y, core), tp: 2 (over x).
Axes of the slice: x: 2, y: 2, z: 4, core: 2. Of those that a mesh axis runs over, the one named last changes fastest.
Arguments:
- resid_in: bfloat16 [65536, 1024], P('dp', 'tp'), may hold values from -6 to 6
- norm_gain: bfloat16 [1024], P('tp'), may hold values from 0.5 to 1.5
- proj_gate: bfloat16 [1024, 2048], P('dp', 'tp'), may hold values from -0.1875 to 0.1875
- proj_value: bfloat16 [1024, 2048], P('dp', 'tp'), may hold values from -0.1875 to 0.1875
- proj_state: bfloat16 [1024, 256], P('dp', 'tp'), may hold values from -0.1875 to 0.1875
- proj_step: bfloat16 [1024, 32], P('dp', 'tp'), may hold values from -0.1875 to 0.1875
- conv_value: float32 [4, 2048], P(None, 'tp'), may hold values from -3 to 3
- value_bias: float32 [2048], P('tp'), may hold values from -3 to 3
- conv_state: float32 [4, 256], P(None, 'tp'), may hold values from -3 to 3
- state_bias: float32 [256], P('tp'), may hold values from -3 to 3
- step_bias: float32 [32], P('tp'), may hold values from -4 to 0
- decay_log: float32 [32], P('tp'), may hold values from -5 to 2.5
- skip_gain: float32 [32], P('tp'), may hold values from 0.2 to 1.2
- gate_gain: float32 [2048], P('tp'), may hold values from 0.5 to 1.5
- proj_out: bfloat16 [2048, 1024], P('tp', 'dp'), may hold values from -0.125 to 0.125
- cotangent: bfloat16 [65536, 1024], P('dp', 'tp'), may hold values from -6 to 6
Outputs:
- block_out: bfloat16 [65536, 1024], P('dp', 'tp')
- grad_in: bfloat16 [65536, 1024], P('dp', 'tp')
- grad_norm_gain: float32 [1024], P('tp')
- grad_proj_gate: float32 [1024, 2048], P('dp', 'tp')
- grad_proj_value: float32 [1024, 2048], P('dp', 'tp')
- grad_proj_state: float32 [1024, 256], P('dp', 'tp')
- grad_proj_step: float32 [1024, 32], P('dp', 'tp')
- grad_conv_value: float32 [4, 2048], P(None, 'tp')
- grad_value_bias: float32 [2048], P('tp')
- grad_conv_state: float32 [4, 256], P(None, 'tp')
- grad_state_bias: float32 [256], P('tp')
- grad_step_bias: float32 [32], P('tp')
- grad_decay_log: float32 [32], P('tp')
- grad_skip_gain: float32 [32], P('tp')
- grad_gate_gain: float32 [2048], P('tp')
- grad_proj_out: float32 [2048, 1024], P('tp', 'dp')
The draws below stay inside these ranges and needn't reach their ends.
All inputs are finite; a program needn't handle non-finite values.
Results may differ from the reference program's by a relative error of at most 0.012.
The reference program's roundings to bfloat16 on the way count: a program that leaves them out, or rounds other values in their place, can miss the bound.
Values may be sent and summed in bfloat16 or wider, within the bound.
A program may use at most 384 MiB of HBM per device.

```python
from functools import partial
import jax
import jax.numpy as jnp
from jax import lax

D = 1024
HEADS = 32
HEADDIM = 64
STATE = 128
CONV = 4
GROUP = 256
SEQ = 2048
INNER = 2048
TOKENS = 65536


def steps_of(own_key, shape, cuts, low, high):
    def one(position, shards_of):
        heights = jax.random.uniform(jax.random.fold_in(jax.random.fold_in(own_key, 6), position), (shards_of,), jnp.float32, low / len(cuts), high / len(cuts))
        return jnp.repeat(jnp.exp(heights), shape[position] // shards_of).reshape((-1,) + (1,) * (len(shape) - position - 1))

    level = one(*cuts[0])
    for cut in cuts[1:]:
        level = level * one(*cut)
    return level


def centred(stream_key, dims, width, limit, cuts=(), kind=jnp.bfloat16):
    factor_of = steps_of(stream_key, dims, cuts, -0.22, 0.18) if cuts else 1.0
    values = jax.random.normal(stream_key, dims, jnp.float32) * width * factor_of
    return jnp.minimum(jnp.maximum(values, -limit), limit).astype(kind)


def setup_inputs(seed: int = 0) -> dict:
    splits = jax.random.split(jax.random.key(seed), 17)
    resid_in = centred(splits[0], (TOKENS, D), 1.0, 6.0, ((0, 16), (1, 2)))
    norm_gain = jnp.clip(0.5 + 1.0 * jax.random.uniform(splits[1], (D,), jnp.float32) ** steps_of(splits[1], (D,), ((0, 2),), -0.2, 0.2), 0.5, 1.5).astype(jnp.bfloat16)
    proj_gate = centred(splits[2], (D, INNER), D ** -0.5, 0.1875, ((0, 16), (1, 2)))
    proj_value = centred(splits[3], (D, INNER), D ** -0.5, 0.1875, ((0, 16), (1, 2)))
    proj_state = centred(splits[4], (D, 2 * STATE), D ** -0.5, 0.1875, ((0, 16), (1, 2)))
    proj_step = centred(splits[5], (D, HEADS), D ** -0.5, 0.1875, ((0, 16), (1, 2)))
    conv_value = centred(splits[6], (CONV, INNER), CONV ** -0.5, 3.0, ((1, 2),), jnp.float32)
    value_bias = centred(splits[7], (INNER,), 0.5, 3.0, ((0, 2),), jnp.float32)
    conv_state = centred(splits[8], (CONV, 2 * STATE), CONV ** -0.5, 3.0, ((1, 2),), jnp.float32)
    state_bias = centred(splits[9], (2 * STATE,), 0.5, 3.0, ((0, 2),), jnp.float32)
    step_bias = jnp.clip(-4.0 + 4.0 * jax.random.uniform(splits[10], (HEADS,), jnp.float32) ** steps_of(splits[10], (HEADS,), ((0, 2),), -0.2, 0.2), -4.0, 0.0)
    decay_log = jnp.clip(-5.0 + 7.5 * jax.random.uniform(splits[11], (HEADS,), jnp.float32) ** steps_of(splits[11], (HEADS,), ((0, 2),), -0.2, 0.2), -5.0, 2.5)
    skip_gain = jnp.clip(0.2 + 1 * jax.random.uniform(splits[12], (HEADS,), jnp.float32) ** steps_of(splits[12], (HEADS,), ((0, 2),), -0.2, 0.2), 0.2, 1.2)
    gate_gain = jnp.clip(0.5 + 1.0 * jax.random.uniform(splits[13], (INNER,), jnp.float32) ** steps_of(splits[13], (INNER,), ((0, 2),), -0.2, 0.2), 0.5, 1.5)
    proj_out = centred(splits[14], (INNER, D), INNER ** -0.5, 0.125, ((0, 2), (1, 16)))
    cotangent = centred(splits[15], (TOKENS, D), 1.0, 6.0, ((0, 16), (1, 2)))
    return {"resid_in": resid_in, "norm_gain": norm_gain, "proj_gate": proj_gate, "proj_value": proj_value, "proj_state": proj_state, "proj_step": proj_step, "conv_value": conv_value, "value_bias": value_bias, "conv_state": conv_state, "state_bias": state_bias, "step_bias": step_bias, "decay_log": decay_log, "skip_gain": skip_gain, "gate_gain": gate_gain, "proj_out": proj_out, "cotangent": cotangent}


epsilon = 1e-05

@jax.custom_vjp
def low(v):
    return lax.optimization_barrier(v.astype(jnp.bfloat16)).astype(jnp.float32)

@jax.custom_vjp
def low_back(v):
    return v

def low_keep(v):
    return (low(v), None)

def low_pass(kept, grad):
    return (grad,)

def back_keep(v):
    return (v, None)

def back_low(kept, grad):
    return (low(grad),)
low.defvjp(low_keep, low_pass)
low_back.defvjp(back_keep, back_low)

def causal_conv(signal, kernel, kernel_bias):
    kernel_len = kernel.shape[0]
    length = signal.shape[0]
    padded = jnp.pad(signal, ((kernel_len - 1, 0), (0, 0)))
    summed = jnp.broadcast_to(kernel_bias[None, :], signal.shape)
    for offset in range(kernel_len):
        summed = summed + kernel[offset][None, :] * padded[offset:offset + length]
    return summed

def group_step(decay_rate, skip_gain, carried, pieces):
    highest = lax.Precision.HIGHEST
    values, step_size, enter_map, read_map = pieces
    block_len = values.shape[0]
    log_decay = jnp.cumsum(step_size * decay_rate[None, :], axis=0)
    lower_mask = jnp.tril(jnp.ones((block_len, block_len), dtype=bool))
    decay_diff = log_decay[:, None, :] - log_decay[None, :, :]
    decay_mask = jnp.exp(jnp.where(lower_mask[:, :, None], decay_diff, -jnp.inf))
    scores = jnp.dot(read_map, enter_map.T, precision=highest)
    weights = scores[:, :, None] * decay_mask * step_size[None, :, :]
    within = jnp.einsum('ijh,jhp->ihp', weights, values, precision=highest)
    across = jnp.einsum('is,hps->ihp', read_map, carried, precision=highest) * jnp.exp(log_decay)[:, :, None]
    to_end = jnp.exp(log_decay[-1][None, :] - log_decay) * step_size
    scaled_values = values * to_end[:, :, None]
    updated = jnp.exp(log_decay[-1])[:, None, None] * carried + jnp.einsum('jhp,js->hps', scaled_values, enter_map, precision=highest)
    result = within + across + skip_gain[None, :, None] * values
    return (updated, result)

def ssd(values, step_size, enter_map, read_map, decay_rate, skip_gain, group_len):
    total_len, head_count, head_dim = values.shape
    state_dim = enter_map.shape[1]
    blocks = total_len // group_len
    pieces = (values.reshape(blocks, group_len, head_count, head_dim), step_size.reshape(blocks, group_len, head_count), enter_map.reshape(blocks, group_len, state_dim), read_map.reshape(blocks, group_len, state_dim))
    start = jnp.zeros((head_count, head_dim, state_dim), values.dtype)
    stepper = jax.checkpoint(partial(group_step, decay_rate, skip_gain))
    finals, outputs = lax.scan(stepper, start, pieces)
    return outputs.reshape(total_len, head_count, head_dim)

def block_forward(params, residual):
    norm_gain, proj_gate, proj_value, proj_state, proj_step, conv_value, value_bias, conv_state, state_bias, step_bias, decay_log, skip_gain, gate_gain, proj_out = params
    highest = lax.Precision.HIGHEST
    meansq = lax.optimization_barrier(jnp.mean(residual * residual, axis=-1, keepdims=True))
    normed_in = low(residual * lax.rsqrt(meansq + epsilon) * norm_gain)
    gate_raw = low_back(jnp.dot(normed_in, proj_gate, precision=highest))
    value_raw = low_back(jnp.dot(normed_in, proj_value, precision=highest))
    state_raw = low_back(jnp.dot(normed_in, proj_state, precision=highest))
    step_raw = low_back(jnp.dot(normed_in, proj_step, precision=highest))
    values = low(jax.nn.silu(causal_conv(value_raw, conv_value, value_bias)))
    maps = low(jax.nn.silu(causal_conv(state_raw, conv_state, state_bias)))
    step_size = jax.nn.softplus(step_raw + step_bias)
    mixed = ssd(values.reshape(SEQ, HEADS, HEADDIM), step_size, maps[:, :STATE], maps[:, STATE:], -jnp.exp(decay_log), skip_gain, GROUP).reshape(SEQ, INNER)
    gated = mixed * jax.nn.silu(gate_raw)
    gate_scale = lax.rsqrt(lax.optimization_barrier(jnp.mean(gated * gated, axis=-1, keepdims=True)) + epsilon)
    normed_out = low(gated * gate_scale * gate_gain)
    return residual + jnp.dot(normed_out, proj_out, precision=highest)

def add_pair(former, latter):
    return former + latter

def reference(resid_in, norm_gain, proj_gate, proj_value, proj_state, proj_step, conv_value, value_bias, conv_state, state_bias, step_bias, decay_log, skip_gain, gate_gain, proj_out, cotangent):
    params = (norm_gain.astype(jnp.float32), proj_gate.astype(jnp.float32), proj_value.astype(jnp.float32), proj_state.astype(jnp.float32), proj_step.astype(jnp.float32), conv_value.astype(jnp.float32), value_bias.astype(jnp.float32), conv_state.astype(jnp.float32), state_bias.astype(jnp.float32), step_bias.astype(jnp.float32), decay_log.astype(jnp.float32), skip_gain.astype(jnp.float32), gate_gain.astype(jnp.float32), proj_out.astype(jnp.float32))
    seq_count = TOKENS // SEQ
    rows_in = resid_in.astype(jnp.float32).reshape(seq_count, SEQ, D)
    rows_back = cotangent.astype(jnp.float32).reshape(seq_count, SEQ, D)

    def one_sequence(totals, item):
        residual, incoming = item
        result, pull = jax.vjp(block_forward, params, residual)
        param_grads, input_grad = pull(incoming)
        totals = jax.tree.map(add_pair, totals, param_grads)
        return (totals, (result.astype(jnp.bfloat16), input_grad.astype(jnp.bfloat16)))
    zeros = jax.tree.map(jnp.zeros_like, params)
    totals, (outputs, input_grads) = lax.scan(one_sequence, zeros, (rows_in, rows_back))
    return (outputs.reshape(TOKENS, D), input_grads.reshape(TOKENS, D), totals[0], totals[1], totals[2], totals[3], totals[4], totals[5], totals[6], totals[7], totals[8], totals[9], totals[10], totals[11], totals[12], totals[13])
```

```python
from functools import partial

import jax
import jax.numpy as jnp
from jax import lax
from jax.experimental import pallas as pl
from jax.experimental.pallas import tpu as pltpu
from jax.sharding import PartitionSpec as P

D = 1024
HEADDIM = 64
GROUP = 256
SEQ = 2048
INNER = 2048


epsilon = 1e-05


def causal_conv(signal, kernel, kernel_bias):
    kernel_len = kernel.shape[0]
    length = signal.shape[0]
    padded = jnp.pad(signal, ((kernel_len - 1, 0), (0, 0)))
    summed = jnp.broadcast_to(kernel_bias[None, :], signal.shape)
    for offset in range(kernel_len):
        summed = summed + kernel[offset][None, :] * padded[offset : offset + length]
    return summed


def group_step(decay_rate, skip_gain, carried, pieces):
    highest = lax.Precision.HIGHEST
    values, step_size, enter_map, read_map = pieces
    block_len = values.shape[0]
    log_decay = jnp.cumsum(step_size * decay_rate[None, :], axis=0)
    lower_mask = jnp.tril(jnp.ones((block_len, block_len), dtype=bool))
    decay_diff = log_decay[:, None, :] - log_decay[None, :, :]
    decay_mask = jnp.exp(jnp.where(lower_mask[:, :, None], decay_diff, -jnp.inf))
    scores = jnp.dot(read_map, enter_map.T, precision=highest)
    weights = scores[:, :, None] * decay_mask * step_size[None, :, :]
    within = jnp.einsum("ijh,jhp->ihp", weights, values, precision=highest)
    across = (
        jnp.einsum("is,hps->ihp", read_map, carried, precision=highest)
        * jnp.exp(log_decay)[:, :, None]
    )
    to_end = jnp.exp(log_decay[-1][None, :] - log_decay) * step_size
    scaled_values = values * to_end[:, :, None]
    updated = jnp.exp(log_decay[-1])[:, None, None] * carried + jnp.einsum(
        "jhp,js->hps", scaled_values, enter_map, precision=highest
    )
    result = within + across + skip_gain[None, :, None] * values
    return (updated, result)


def ssd(values, step_size, enter_map, read_map, decay_rate, skip_gain, group_len):
    total_len, head_count, head_dim = values.shape
    state_dim = enter_map.shape[1]
    blocks = total_len // group_len
    pieces = (
        values.reshape(blocks, group_len, head_count, head_dim),
        step_size.reshape(blocks, group_len, head_count),
        enter_map.reshape(blocks, group_len, state_dim),
        read_map.reshape(blocks, group_len, state_dim),
    )
    start = jnp.zeros((head_count, head_dim, state_dim), values.dtype)
    stepper = jax.checkpoint(partial(group_step, decay_rate, skip_gain))
    finals, outputs = lax.scan(stepper, start, pieces)
    return outputs.reshape(total_len, head_count, head_dim)


def product(matrix, factor):
    return jnp.dot(matrix, factor, preferred_element_type=jnp.float32)


def product_left(matrix, factor):
    return jnp.einsum("tk,tc->kc", matrix, factor, preferred_element_type=jnp.float32)


def product_right(matrix, factor):
    return jnp.einsum("tc,kc->tk", matrix, factor, preferred_element_type=jnp.float32)


def gating(mixed_in, gate_in):
    return mixed_in * jax.nn.silu(gate_in)


def by_heads(
    resid_in,
    norm_gain,
    proj_gate,
    proj_value,
    proj_state,
    proj_step,
    conv_value,
    value_bias,
    conv_state,
    state_bias,
    step_bias,
    decay_log,
    skip_gain,
    gate_gain,
    proj_out,
    cotangent,
):
    resid_full, gain_row, cot_full = (
        lax.all_gather(resid_in, "tp", axis=1, tiled=True),
        lax.all_gather(norm_gain[None, :], "tp", axis=1, tiled=True),
        lax.all_gather(cotangent, "tp", axis=1, tiled=True),
    )
    gate_w, value_w, state_w, step_w, out_w = (
        lax.all_gather(proj_gate, "dp", axis=0, tiled=True),
        lax.all_gather(proj_value, "dp", axis=0, tiled=True),
        lax.all_gather(proj_state, "dp", axis=0, tiled=True),
        lax.all_gather(proj_step, "dp", axis=0, tiled=True),
        lax.all_gather(proj_out, "dp", axis=1, tiled=True),
    )
    resid_wide = resid_full.astype(jnp.float32)
    inv_rms = lax.rsqrt(jnp.mean(resid_wide * resid_wide, axis=-1, keepdims=True) + epsilon)
    unit_rows = resid_wide * inv_rms
    gain_wide = gain_row.astype(jnp.float32)
    normed_in = (unit_rows * gain_wide).astype(jnp.bfloat16)
    gate_raw = product(normed_in, gate_w)
    value_raw = product(normed_in, value_w)
    state_raw = product(normed_in, state_w)
    step_raw = product(normed_in, step_w)
    seq_count = resid_in.shape[0] // SEQ

    def conv_act(raw, kernel, kernel_bias):
        framed = raw.reshape(seq_count, SEQ, raw.shape[1])
        convolved = jax.vmap(causal_conv, (0, None, None))(framed, kernel, kernel_bias)
        return jax.nn.silu(convolved).reshape(raw.shape)

    value_act, value_pull = jax.vjp(conv_act, value_raw, conv_value, value_bias)
    values = value_act.astype(jnp.bfloat16)
    state_act, state_pull = jax.vjp(conv_act, state_raw, conv_state, state_bias)
    maps = lax.all_gather(state_act.astype(jnp.bfloat16), "tp", axis=1, tiled=True)
    head_count = step_raw.shape[1]
    state_dim = maps.shape[1] // 2

    def mixer(values_in, maps_in, step_in, bias_in, log_in, skip_in):
        step_size = jax.nn.softplus(step_in + bias_in)
        scan_one = partial(ssd, group_len=GROUP)
        mixed_out = jax.vmap(scan_one, (0, 0, 0, 0, None, None))(
            values_in.reshape(seq_count, SEQ, head_count, HEADDIM),
            step_size.reshape(seq_count, SEQ, head_count),
            maps_in[:, :state_dim].reshape(seq_count, SEQ, state_dim),
            maps_in[:, state_dim:].reshape(seq_count, SEQ, state_dim),
            -jnp.exp(log_in),
            skip_in,
        )
        return mixed_out.reshape(values_in.shape)

    mixed, mixer_pull = jax.vjp(
        mixer,
        values.astype(jnp.float32),
        maps.astype(jnp.float32),
        step_raw,
        step_bias,
        decay_log,
        skip_gain,
    )
    gated, gate_pull = jax.vjp(gating, mixed, gate_raw)
    squares = lax.psum(jnp.sum(gated * gated, axis=-1), "tp")
    gate_scale = lax.rsqrt(squares / INNER + epsilon)[:, None]
    scaled = gated * gate_scale
    normed_out = (scaled * gate_gain).astype(jnp.bfloat16)
    out_terms = product(normed_out, out_w)
    out_mine = lax.psum_scatter(out_terms, "tp", scatter_dimension=1, tiled=True)
    block_out = (resid_in.astype(jnp.float32) + out_mine).astype(jnp.bfloat16)
    normed_grad = product_right(cot_full, out_w)
    out_grad = product_left(normed_out, cot_full)
    gate_gain_grad = jnp.sum(normed_grad * scaled, axis=0)
    weighted = normed_grad * gate_gain
    crossed = lax.psum(jnp.sum(weighted * gated, axis=-1), "tp")
    cubed = gate_scale * gate_scale * gate_scale
    gated_grad = weighted * gate_scale - gated * cubed * (crossed[:, None] / INNER)
    mixed_grad, gate_raw_grad = gate_pull(gated_grad)
    values_grad, maps_grad, step_grad, step_bias_grad, decay_grad, skip_grad = mixer_pull(
        mixed_grad
    )
    maps_mine = lax.psum_scatter(maps_grad, "tp", scatter_dimension=1, tiled=True)
    value_raw_grad, conv_value_grad, value_bias_grad = value_pull(values_grad)
    state_raw_grad, conv_state_grad, state_bias_grad = state_pull(maps_mine)
    gate_low = gate_raw_grad.astype(jnp.bfloat16)
    value_low = value_raw_grad.astype(jnp.bfloat16)
    state_low = state_raw_grad.astype(jnp.bfloat16)
    step_low = step_grad.astype(jnp.bfloat16)
    gate_w_grad = product_left(normed_in, gate_low)
    value_w_grad = product_left(normed_in, value_low)
    state_w_grad = product_left(normed_in, state_low)
    step_w_grad = product_left(normed_in, step_low)
    input_terms = (
        product_right(gate_low, gate_w)
        + product_right(value_low, value_w)
        + product_right(state_low, state_w)
        + product_right(step_low, step_w)
    )
    width_mine = resid_in.shape[1]
    start = lax.axis_index("tp") * width_mine
    unit_mine = lax.dynamic_slice_in_dim(unit_rows, start, width_mine, 1)
    resid_mine = resid_in.astype(jnp.float32)
    gain_mine = norm_gain.astype(jnp.float32)
    input_whole = lax.psum(input_terms, "tp")
    crossed_rows = jnp.sum(input_whole * gain_wide * resid_wide, axis=-1)
    input_mine = lax.dynamic_slice_in_dim(input_whole, start, width_mine, 1)
    pulled = input_mine * gain_mine
    rms_cubed = inv_rms * inv_rms * inv_rms
    grad_in = (
        cotangent.astype(jnp.float32)
        + pulled * inv_rms
        - resid_mine * rms_cubed * (crossed_rows[:, None] / D)
    ).astype(jnp.bfloat16)
    gain_grad = jnp.sum(input_mine * unit_mine, axis=0)
    large_sums = (
        lax.psum_scatter(gate_w_grad, "dp", scatter_dimension=0, tiled=True),
        lax.psum_scatter(value_w_grad, "dp", scatter_dimension=0, tiled=True),
        lax.psum_scatter(state_w_grad, "dp", scatter_dimension=0, tiled=True),
        lax.psum_scatter(step_w_grad, "dp", scatter_dimension=0, tiled=True),
        lax.psum_scatter(out_grad, "dp", scatter_dimension=1, tiled=True),
    )
    small_sums = lax.psum(
        (
            gain_grad,
            conv_value_grad,
            value_bias_grad,
            conv_state_grad,
            state_bias_grad,
            step_bias_grad,
            decay_grad,
            skip_grad,
            gate_gain_grad,
        ),
        "dp",
    )
    return (
        block_out,
        grad_in,
        small_sums[0],
        large_sums[0],
        large_sums[1],
        large_sums[2],
        large_sums[3],
        small_sums[1],
        small_sums[2],
        small_sums[3],
        small_sums[4],
        small_sums[5],
        small_sums[6],
        small_sums[7],
        small_sums[8],
        large_sums[4],
    )


CHUNK = 128
QUAD = 8
WIDE = QUAD * HEADDIM
F32 = jnp.float32
BF16 = jnp.bfloat16


def nt(left, right):
    return lax.dot_general(left, right, (((1,), (1,)), ((), ())), preferred_element_type=F32)


def nn(left, right):
    return jnp.dot(left, right, preferred_element_type=F32)


def parts(v):
    high = v.astype(BF16)
    return high, (v - high.astype(F32)).astype(BF16)


def twice(v, axis=1):
    return jnp.concatenate([v, v], axis=axis)


def stacked(pair, axis=0):
    return jnp.concatenate(pair, axis=axis)


def nt_parts(left, right):
    return nt(left[0], right[0]) + nt(left[0], right[1]) + nt(left[1], right[0])


def pair_columns(ref, pair, lane_low):
    first = jnp.broadcast_to(ref[0, :, 2 * pair : 2 * pair + 1], (CHUNK, 128))
    second = jnp.broadcast_to(ref[0, :, 2 * pair + 1 : 2 * pair + 2], (CHUNK, 128))
    return first, second, jnp.where(lane_low, first, second)


def two_heads(block, lane_low):
    zero = jnp.zeros_like(block)
    return jnp.concatenate([jnp.where(lane_low, block, zero), jnp.where(lane_low, zero, block)], axis=0)


def scan_forward(per_seq, x_ref, b_ref, c_ref, bt_ref, acol_ref, dtcol_ref, arow_ref, skip_ref, y_ref, st_ref, state, scores):
    step, quad = pl.program_id(0), pl.program_id(1)
    row = lax.broadcasted_iota(jnp.int32, (CHUNK, CHUNK), 0)
    col = lax.broadcasted_iota(jnp.int32, (CHUNK, CHUNK), 1)
    lane_low = col < HEADDIM

    @pl.when(lax.rem(step, per_seq) == 0)
    def _():
        state[quad] = jnp.zeros((CHUNK, WIDE), F32)

    @pl.when(quad == 0)
    def _():
        scores[...] = jnp.where(row >= col, nt(c_ref[...], b_ref[...]), 0.0)

    entering = state[quad]
    st_ref[0] = entering
    across = nn(twice(c_ref[...]), stacked(parts(entering)))
    within = scores[...]
    ends, rights = [], []
    for pair in range(QUAD // 2):
        lanes = slice(128 * pair, 128 * pair + 128)
        x = x_ref[:, lanes].astype(F32)
        a1, a2, asel = pair_columns(acol_ref, pair, lane_low)
        _, _, dsel = pair_columns(dtcol_ref, pair, lane_low)
        u = x * dsel
        m1 = within * jnp.exp(jnp.minimum(a1 - arow_ref[0, 2 * pair : 2 * pair + 1, :], 0.0))
        m2 = within * jnp.exp(jnp.minimum(a2 - arow_ref[0, 2 * pair + 1 : 2 * pair + 2, :], 0.0))
        both = jnp.concatenate([m1.astype(BF16), m2.astype(BF16)], axis=1)
        y = nn(both, two_heads(u.astype(BF16), lane_low))
        y_ref[:, lanes] = y + jnp.exp(asel) * across[:, lanes] + skip_ref[:, lanes] * x
        last = asel[CHUNK - 1 : CHUNK, :]
        rights.append(jnp.exp(last - asel) * u)
        ends.append(jnp.exp(last))
    added = nn(twice(bt_ref[...]), stacked(parts(jnp.concatenate(rights, axis=1))))
    state[quad] = jnp.concatenate(ends, axis=1) * entering + added


def scan_backward(per_seq, quads, x_ref, dy_ref, b_ref, c_ref, ct_ref, acol_ref, dtcol_ref, arow_ref, skip_ref, st_ref, pick_ref,
                  dx_ref, db_ref, dc_ref, small_ref, dskip_ref, grads, scores, scores_t, dscores):
    step, quad = pl.program_id(0), pl.program_id(1)
    row = lax.broadcasted_iota(jnp.int32, (CHUNK, CHUNK), 0)
    col = lax.broadcasted_iota(jnp.int32, (CHUNK, CHUNK), 1)
    lane_low = col < HEADDIM

    @pl.when(lax.rem(step, per_seq) == 0)
    def _():
        grads[quad] = jnp.zeros((CHUNK, WIDE), F32)

    @pl.when(quad == 0)
    def _():
        scores[...] = jnp.where(row >= col, nt(c_ref[...], b_ref[...]), 0.0)
        scores_t[...] = jnp.where(row <= col, nt(b_ref[...], c_ref[...]), 0.0)
        dscores[...] = jnp.zeros_like(dscores)
        db_ref[...] = jnp.zeros_like(db_ref)
        dc_ref[...] = jnp.zeros_like(dc_ref)

    leaving = grads[quad]
    leaving_parts = parts(leaving)
    entering = st_ref[0]
    entering_parts = parts(entering)
    across = nn(twice(c_ref[...]), stacked(entering_parts))
    from_state = nn(twice(b_ref[...]), stacked(leaving_parts))
    kept = jnp.sum(leaving * entering, axis=0, keepdims=True)
    within, within_t = scores[...], scores_t[...]
    dwithin = jnp.zeros((CHUNK, CHUNK), F32)
    ends, rights, reads, his, los, steps = [], [], [], [], [], []
    for pair in range(QUAD // 2):
        lanes = slice(128 * pair, 128 * pair + 128)
        x = x_ref[:, lanes].astype(F32)
        dy = dy_ref[:, lanes]
        dy_low = dy.astype(BF16)
        dy_back = dy_low.astype(F32)
        a1, a2, asel = pair_columns(acol_ref, pair, lane_low)
        _, _, dsel = pair_columns(dtcol_ref, pair, lane_low)
        r1 = arow_ref[0, 2 * pair : 2 * pair + 1, :]
        r2 = arow_ref[0, 2 * pair + 1 : 2 * pair + 2, :]
        d1, d2 = a1 - r1, a2 - r2
        l1, l2 = jnp.exp(jnp.minimum(d1, 0.0)), jnp.exp(jnp.minimum(d2, 0.0))
        t1, t2 = jnp.exp(jnp.minimum(-d1, 0.0)), jnp.exp(jnp.minimum(-d2, 0.0))
        u = x * dsel
        u_low = u.astype(BF16)
        u_back = u_low.astype(F32)
        dy_two = two_heads(dy_low, lane_low)
        both = jnp.concatenate([(within * l1).astype(BF16), (within * l2).astype(BF16)], axis=1)
        both_t = jnp.concatenate([(within_t * t1).astype(BF16), (within_t * t2).astype(BF16)], axis=1)
        y = nn(both, two_heads(u_low, lane_low))
        du = nn(both_t, dy_two)
        w = nt(stacked((dy_two, two_heads((dy - dy_back).astype(BF16), lane_low)), 1), twice(u_low))
        dwithin = dwithin + l1 * w[:CHUNK] + l2 * w[CHUNK:]
        last = asel[CHUNK - 1 : CHUNK, :]
        last_decay = jnp.exp(last)
        into = jnp.exp(asel)
        out_of = jnp.exp(last - asel)
        du_state = out_of * from_state[:, lanes]
        du_all = du + du_state
        dx_ref[:, lanes] = dsel * du_all + skip_ref[:, lanes] * dy
        passed = u * du_state
        final = jnp.sum(passed, axis=0, keepdims=True) + last_decay * kept[:, lanes]
        read = dy * into
        da = dy_back * y + read * across[:, lanes] - u_back * du - passed
        da = da + jnp.where(row == CHUNK - 1, final, 0.0)
        da_hi = da.astype(BF16)
        his.append(da_hi)
        los.append((da - da_hi.astype(F32)).astype(BF16))
        steps.append((x * du_all).astype(BF16))
        reads.append(read)
        rights.append(out_of * u)
        ends.append(last_decay)
        dskip_ref[0, :, lanes] = jnp.sum((dy * x).reshape(CHUNK // 8, 8, 128), axis=0)
    read = parts(jnp.concatenate(reads, axis=1))
    right = parts(jnp.concatenate(rights, axis=1))
    dscores[...] += dwithin
    dc_ref[...] += nt_parts(read, entering_parts)
    db_ref[...] += nt_parts(right, leaving_parts)
    grads[quad] = jnp.concatenate(ends, axis=1) * leaving + nn(twice(ct_ref[...]), stacked(read))
    small_ref[0] = nn(jnp.concatenate(his + los + steps, axis=1), pick_ref[...])

    @pl.when(quad == quads - 1)
    def _():
        total = jnp.where(row >= col, dscores[...], 0.0)
        dc_ref[...] += nn(stacked(parts(total), 1), twice(b_ref[...], 0))
        db_ref[...] += nn(stacked(parts(total.T), 1), twice(c_ref[...], 0))


def scan_inputs(maps, log_decay, step_size):
    tokens, heads = step_size.shape
    quads = heads // QUAD
    columns = lambda v: v.reshape(tokens, quads, QUAD).transpose(1, 0, 2)
    rows = log_decay.T.reshape(quads, QUAD, tokens)
    half = maps.shape[1] // 2
    return maps[:, :half], maps[:, half:], columns(log_decay), columns(step_size), rows


def run_forward(values, maps, log_decay, step_size, skip_lanes):
    tokens, inner = values.shape
    quads, chunks = inner // WIDE, tokens // CHUNK
    enter, read, acol, dtcol, arow = scan_inputs(maps, log_decay, step_size)
    tall = lambda: pl.BlockSpec((CHUNK, WIDE), lambda i, q: (i, q))
    thin = lambda: pl.BlockSpec((CHUNK, CHUNK), lambda i, q: (i, 0))
    cols = lambda: pl.BlockSpec((1, CHUNK, QUAD), lambda i, q: (q, i, 0))
    return pl.pallas_call(
        partial(scan_forward, SEQ // CHUNK),
        grid=(chunks, quads),
        in_specs=[tall(), thin(), thin(), pl.BlockSpec((CHUNK, CHUNK), lambda i, q: (0, i)), cols(), cols(),
                  pl.BlockSpec((1, QUAD, CHUNK), lambda i, q: (q, 0, i)), pl.BlockSpec((1, WIDE), lambda i, q: (0, q))],
        out_specs=[tall(), pl.BlockSpec((1, CHUNK, WIDE), lambda i, q: (i, 0, q))],
        out_shape=[jax.ShapeDtypeStruct((tokens, inner), F32), jax.ShapeDtypeStruct((chunks, CHUNK, inner), F32)],
        scratch_shapes=[pltpu.VMEM((quads, CHUNK, WIDE), F32), pltpu.VMEM((CHUNK, CHUNK), F32)],
        compiler_params=pltpu.CompilerParams(vmem_limit_bytes=32 * 2**20),
        cost_estimate=pl.CostEstimate(flops=tokens * inner * 1024, bytes_accessed=tokens * inner * 10, transcendentals=tokens * inner * 4),
        name="scan_forward",
    )(values, enter, read, enter.T, acol, dtcol, arow, skip_lanes)


def run_backward(values, dmixed, maps, log_decay, step_size, skip_lanes, states):
    tokens, inner = values.shape
    quads, chunks = inner // WIDE, tokens // CHUNK
    enter, read, acol, dtcol, arow = scan_inputs(maps, log_decay, step_size)
    lane_head = jnp.arange(WIDE)[:, None] // HEADDIM
    pick = lambda base: (lane_head + base == jnp.arange(128)[None, :]).astype(BF16)
    picks = jnp.concatenate([pick(0), pick(0), pick(QUAD)], axis=0)
    end = chunks - 1
    tall = lambda: pl.BlockSpec((CHUNK, WIDE), lambda i, q: (end - i, q))
    thin = lambda: pl.BlockSpec((CHUNK, CHUNK), lambda i, q: (end - i, 0))
    cols = lambda: pl.BlockSpec((1, CHUNK, QUAD), lambda i, q: (q, end - i, 0))
    dx, db, dc, small, dskip = pl.pallas_call(
        partial(scan_backward, SEQ // CHUNK, quads),
        grid=(chunks, quads),
        in_specs=[tall(), tall(), thin(), thin(), pl.BlockSpec((CHUNK, CHUNK), lambda i, q: (0, end - i)), cols(), cols(),
                  pl.BlockSpec((1, QUAD, CHUNK), lambda i, q: (q, 0, end - i)), pl.BlockSpec((1, WIDE), lambda i, q: (0, q)),
                  pl.BlockSpec((1, CHUNK, WIDE), lambda i, q: (end - i, 0, q)), pl.BlockSpec((3 * WIDE, 128), lambda i, q: (0, 0))],
        out_specs=[tall(), thin(), thin(), pl.BlockSpec((1, CHUNK, 128), lambda i, q: (q, end - i, 0)),
                   pl.BlockSpec((1, 8, WIDE), lambda i, q: (end - i, 0, q))],
        out_shape=[jax.ShapeDtypeStruct((tokens, inner), F32), jax.ShapeDtypeStruct((tokens, CHUNK), F32),
                   jax.ShapeDtypeStruct((tokens, CHUNK), F32), jax.ShapeDtypeStruct((quads, tokens, 128), F32),
                   jax.ShapeDtypeStruct((chunks, 8, inner), F32)],
        scratch_shapes=[pltpu.VMEM((quads, CHUNK, WIDE), F32)] + [pltpu.VMEM((CHUNK, CHUNK), F32)] * 3,
        compiler_params=pltpu.CompilerParams(vmem_limit_bytes=32 * 2**20),
        cost_estimate=pl.CostEstimate(flops=tokens * inner * 2560, bytes_accessed=tokens * inner * 12, transcendentals=tokens * inner * 8),
        name="scan_backward",
    )(values, dmixed, enter, read, read.T, acol, dtcol, arow, skip_lanes, states, picks)
    per_head = lambda part: part.transpose(1, 0, 2).reshape(tokens, quads * QUAD)
    dlog = per_head(small[:, :, :QUAD])
    dstep = per_head(small[:, :, QUAD : 2 * QUAD])
    dskip = jnp.sum(dskip.reshape(chunks * 8, inner // HEADDIM, HEADDIM), axis=(0, 2))
    return dx, jnp.concatenate([db, dc], axis=1), dlog, dstep, dskip


def chunk_sums(v, lower):
    tokens, heads = v.shape
    framed = v.reshape(tokens // CHUNK, CHUNK, heads)
    ones = jnp.tril(jnp.ones((CHUNK, CHUNK), F32))
    ones = ones if lower else ones.T
    return jnp.einsum("ts,csh->cth", ones, framed, precision=lax.Precision.HIGHEST).reshape(tokens, heads)


def to_sequences(block):
    me = lax.axis_index("tp")
    rows = block.shape[0] // 2
    mine = lax.dynamic_slice_in_dim(block, me * rows, rows, 0)
    other = lax.dynamic_slice_in_dim(block, (1 - me) * rows, rows, 0)
    came = lax.ppermute(other, "tp", [(0, 1), (1, 0)])
    first = me == 0
    return jnp.concatenate([jnp.where(first, mine, came), jnp.where(first, came, mine)], axis=1)


def to_features(block):
    me = lax.axis_index("tp")
    cols = block.shape[1] // 2
    mine = lax.dynamic_slice_in_dim(block, me * cols, cols, 1)
    other = lax.dynamic_slice_in_dim(block, (1 - me) * cols, cols, 1)
    came = lax.ppermute(other, "tp", [(0, 1), (1, 0)])
    first = me == 0
    return jnp.concatenate([jnp.where(first, mine, came), jnp.where(first, came, mine)], axis=0)


def gather_columns(shards):
    widths = [shard.shape[1] for shard in shards]
    wide = lax.all_gather(jnp.concatenate(shards, axis=1), "tp", axis=0)
    pieces, at = [], 0
    for width in widths:
        pieces += [wide[part, :, at : at + width] for part in range(wide.shape[0])]
        at += width
    return lax.all_gather(jnp.concatenate(pieces, axis=1), "dp", axis=0, tiled=True)


def scatter_columns(whole, widths, tp):
    rows = lax.psum_scatter(whole, "dp", scatter_dimension=0, tiled=True)
    pieces, at = [], 0
    for width in widths:
        pieces.append(rows[:, at : at + width * tp].reshape(rows.shape[0], tp, width))
        at += width * tp
    mine = lax.psum_scatter(jnp.concatenate(pieces, axis=2).transpose(1, 0, 2), "tp", scatter_dimension=0, tiled=True)[0]
    outs, at = [], 0
    for width in widths:
        outs.append(mine[:, at : at + width])
        at += width
    return outs


def by_sequences(
    tp,
    resid_in,
    norm_gain,
    proj_gate,
    proj_value,
    proj_state,
    proj_step,
    conv_value,
    value_bias,
    conv_state,
    state_bias,
    step_bias,
    decay_log,
    skip_gain,
    gate_gain,
    proj_out,
    cotangent,
):
    small_in = [norm_gain.astype(F32), conv_value, value_bias, conv_state, state_bias, step_bias, decay_log, skip_gain, gate_gain]
    packed = lax.all_gather(jnp.concatenate([v.reshape(-1) for v in small_in]), "tp", axis=0)
    fulls, at = [], 0
    for v in small_in:
        piece = packed[:, at : at + v.size].reshape((tp,) + v.shape)
        at += v.size
        fulls.append(piece.reshape(-1) if v.ndim == 1 else piece.transpose(1, 0, 2).reshape(v.shape[0], -1))
    gain, conv_v, bias_v, conv_s, bias_s, bias_step, log_rate, skip, gain_out = fulls

    resid = to_sequences(resid_in).astype(F32)
    low_w = gather_columns([proj_value, proj_state, proj_step])
    gate_w = gather_columns([proj_gate])
    out_rows = lax.all_gather(proj_out, "tp", axis=0, tiled=True)
    out_w = lax.all_gather(out_rows, "dp", axis=1, tiled=True)
    cot_low = to_sequences(cotangent)

    tokens = resid.shape[0]
    seqs = tokens // SEQ
    inner = gate_w.shape[1]
    states = conv_s.shape[1]
    value_w, rest_w = low_w[:, :inner], low_w[:, inner:]

    inv_rms = lax.rsqrt(jnp.mean(resid * resid, axis=-1, keepdims=True) + epsilon)
    unit_rows = resid * inv_rms
    normed_in = (unit_rows * gain).astype(BF16)
    value_raw = product(normed_in, value_w)
    rest_raw = product(normed_in, rest_w)
    state_raw, step_raw = rest_raw[:, :states], rest_raw[:, states:]

    def conv_act(raw, kernel, kernel_bias):
        framed = raw.reshape(seqs, SEQ, raw.shape[1])
        convolved = jax.vmap(causal_conv, (0, None, None))(framed, kernel, kernel_bias)
        return jax.nn.silu(convolved).reshape(raw.shape)

    value_act, value_pull = jax.vjp(conv_act, value_raw, conv_v, bias_v)
    values = value_act.astype(BF16)
    state_act, state_pull = jax.vjp(conv_act, state_raw, conv_s, bias_s)
    maps = state_act.astype(BF16)
    step_size, step_pull = jax.vjp(lambda v: jax.nn.softplus(v + bias_step), step_raw)
    rate = -jnp.exp(log_rate)
    log_decay = chunk_sums(step_size * rate, True)
    skip_lanes = jnp.repeat(skip, HEADDIM)[None, :]
    mixed, entering = run_forward(values, maps, log_decay, step_size, skip_lanes)

    gate_raw = product(normed_in, gate_w)
    gated, gate_pull = jax.vjp(gating, mixed, gate_raw)
    squares = jnp.sum(gated * gated, axis=-1, keepdims=True)
    gate_scale = lax.rsqrt(squares / inner + epsilon)
    scaled = gated * gate_scale
    normed_out = (scaled * gain_out).astype(BF16)
    block_out = to_features((resid + product(normed_out, out_w)).astype(BF16))
    normed_grad = product_right(cot_low, out_w)
    out_grad = product_left(normed_out, cot_low)
    gate_gain_grad = jnp.sum(normed_grad * scaled, axis=0)
    weighted = normed_grad * gain_out
    crossed = jnp.sum(weighted * gated, axis=-1, keepdims=True)
    cubed = gate_scale * gate_scale * gate_scale
    gated_grad = weighted * gate_scale - gated * cubed * (crossed / inner)
    mixed_grad, gate_raw_grad = gate_pull(gated_grad)
    gate_low = gate_raw_grad.astype(BF16)
    gate_w_grad = product_left(normed_in, gate_low)
    mixed_grad, gate_w_grad, out_grad = lax.optimization_barrier((mixed_grad, gate_w_grad, out_grad))

    values_grad, maps_grad, dlog, dstep, skip_grad = run_backward(
        values, mixed_grad, maps, log_decay, step_size, skip_lanes, entering
    )
    summed = chunk_sums(dlog, False)
    decay_grad = rate * jnp.sum(summed * step_size, axis=0)
    (step_grad,) = step_pull(dstep + summed * rate)
    step_bias_grad = jnp.sum(step_grad, axis=0)
    value_raw_grad, conv_value_grad, value_bias_grad = value_pull(values_grad)
    state_raw_grad, conv_state_grad, state_bias_grad = state_pull(maps_grad)
    rest_low = jnp.concatenate([state_raw_grad.astype(BF16), step_grad.astype(BF16)], axis=1)
    value_low = value_raw_grad.astype(BF16)
    value_w_grad = product_left(normed_in, value_low)
    rest_w_grad = product_left(normed_in, rest_low)
    input_grad = (
        product_right(gate_low, gate_w) + product_right(value_low, value_w) + product_right(rest_low, rest_w)
    )
    gain_grad = jnp.sum(input_grad * unit_rows, axis=0)
    pulled = input_grad * gain
    crossed_rows = jnp.sum(pulled * resid, axis=-1, keepdims=True)
    rms_cubed = inv_rms * inv_rms * inv_rms
    grad_in = (
        cot_low.astype(F32) + pulled * inv_rms - resid * rms_cubed * (crossed_rows / resid.shape[1])
    ).astype(BF16)
    grad_in = to_features(grad_in)

    (gate_mine,) = scatter_columns(gate_w_grad, [proj_gate.shape[1]], tp)
    value_mine, state_mine, step_mine = scatter_columns(
        jnp.concatenate([value_w_grad, rest_w_grad], axis=1),
        [proj_value.shape[1], proj_state.shape[1], proj_step.shape[1]],
        tp,
    )
    out_cols = lax.psum_scatter(out_grad, "dp", scatter_dimension=1, tiled=True)
    out_mine = lax.psum_scatter(out_cols, "tp", scatter_dimension=0, tiled=True)

    small_out = [gain_grad, conv_value_grad, value_bias_grad, conv_state_grad, state_bias_grad, step_bias_grad, decay_grad, skip_grad, gate_gain_grad]
    split = [
        v.reshape(tp, -1) if v.ndim == 1 else v.reshape(v.shape[0], tp, -1).transpose(1, 0, 2).reshape(tp, -1)
        for v in small_out
    ]
    sums = lax.psum(jnp.concatenate(split, axis=1), ("dp", "tp"))
    mine = lax.dynamic_slice_in_dim(sums, lax.axis_index("tp"), 1, 0)[0]
    smalls, at = [], 0
    for v in small_in:
        smalls.append(mine[at : at + v.size].reshape(v.shape))
        at += v.size
    return (
        block_out,
        grad_in,
        smalls[0],
        gate_mine,
        value_mine,
        state_mine,
        step_mine,
        *smalls[1:],
        out_mine,
    )


def solution(mesh):
    tp = mesh.shape["tp"]

    def local(*args):
        seqs = args[0].shape[0] // SEQ
        if seqs % tp == 0 and tp == 2:
            return by_sequences(tp, *args)
        return by_heads(*args)

    return jax.shard_map(
        local,
        mesh=mesh,
        in_specs=(
            P("dp", "tp"),
            P("tp"),
            P("dp", "tp"),
            P("dp", "tp"),
            P("dp", "tp"),
            P("dp", "tp"),
            P(None, "tp"),
            P("tp"),
            P(None, "tp"),
            P("tp"),
            P("tp"),
            P("tp"),
            P("tp"),
            P("tp"),
            P("tp", "dp"),
            P("dp", "tp"),
        ),
        out_specs=(
            P("dp", "tp"),
            P("dp", "tp"),
            P("tp"),
            P("dp", "tp"),
            P("dp", "tp"),
            P("dp", "tp"),
            P("dp", "tp"),
            P(None, "tp"),
            P("tp"),
            P(None, "tp"),
            P("tp"),
            P("tp"),
            P("tp"),
            P("tp"),
            P("tp"),
            P("tp", "dp"),
        ),
        check_vma=False,
    )
```

```python
from functools import partial

import jax
import jax.numpy as jnp
from jax import lax
from jax.experimental import pallas as pl
from jax.experimental.pallas import tpu as pltpu
from jax.sharding import PartitionSpec as P

D = 1024
HEADDIM = 64
GROUP = 256
SEQ = 2048
INNER = 2048


epsilon = 1e-05


def causal_conv(signal, kernel, kernel_bias):
    kernel_len = kernel.shape[0]
    length = signal.shape[0]
    padded = jnp.pad(signal, ((kernel_len - 1, 0), (0, 0)))
    summed = jnp.broadcast_to(kernel_bias[None, :], signal.shape)
    for offset in range(kernel_len):
        summed = summed + kernel[offset][None, :] * padded[offset : offset + length]
    return summed


def group_step(decay_rate, skip_gain, carried, pieces):
    highest = lax.Precision.HIGHEST
    values, step_size, enter_map, read_map = pieces
    block_len = values.shape[0]
    log_decay = jnp.cumsum(step_size * decay_rate[None, :], axis=0)
    lower_mask = jnp.tril(jnp.ones((block_len, block_len), dtype=bool))
    decay_diff = log_decay[:, None, :] - log_decay[None, :, :]
    decay_mask = jnp.exp(jnp.where(lower_mask[:, :, None], decay_diff, -jnp.inf))
    scores = jnp.dot(read_map, enter_map.T, precision=highest)
    weights = scores[:, :, None] * decay_mask * step_size[None, :, :]
    within = jnp.einsum("ijh,jhp->ihp", weights, values, precision=highest)
    across = (
        jnp.einsum("is,hps->ihp", read_map, carried, precision=highest)
        * jnp.exp(log_decay)[:, :, None]
    )
    to_end = jnp.exp(log_decay[-1][None, :] - log_decay) * step_size
    scaled_values = values * to_end[:, :, None]
    updated = jnp.exp(log_decay[-1])[:, None, None] * carried + jnp.einsum(
        "jhp,js->hps", scaled_values, enter_map, precision=highest
    )
    result = within + across + skip_gain[None, :, None] * values
    return (updated, result)


def ssd(values, step_size, enter_map, read_map, decay_rate, skip_gain, group_len):
    total_len, head_count, head_dim = values.shape
    state_dim = enter_map.shape[1]
    blocks = total_len // group_len
    pieces = (
        values.reshape(blocks, group_len, head_count, head_dim),
        step_size.reshape(blocks, group_len, head_count),
        enter_map.reshape(blocks, group_len, state_dim),
        read_map.reshape(blocks, group_len, state_dim),
    )
    start = jnp.zeros((head_count, head_dim, state_dim), values.dtype)
    stepper = jax.checkpoint(partial(group_step, decay_rate, skip_gain))
    finals, outputs = lax.scan(stepper, start, pieces)
    return outputs.reshape(total_len, head_count, head_dim)


def product(matrix, factor):
    return jnp.dot(matrix, factor, preferred_element_type=jnp.float32)


def product_left(matrix, factor):
    return jnp.einsum("tk,tc->kc", matrix, factor, preferred_element_type=jnp.float32)


def product_right(matrix, factor):
    return jnp.einsum("tc,kc->tk", matrix, factor, preferred_element_type=jnp.float32)


def gating(mixed_in, gate_in):
    return mixed_in * jax.nn.silu(gate_in)


def by_heads(
    resid_in,
    norm_gain,
    proj_gate,
    proj_value,
    proj_state,
    proj_step,
    conv_value,
    value_bias,
    conv_state,
    state_bias,
    step_bias,
    decay_log,
    skip_gain,
    gate_gain,
    proj_out,
    cotangent,
):
    resid_full, gain_row, cot_full = (
        lax.all_gather(resid_in, "tp", axis=1, tiled=True),
        lax.all_gather(norm_gain[None, :], "tp", axis=1, tiled=True),
        lax.all_gather(cotangent, "tp", axis=1, tiled=True),
    )
    gate_w, value_w, state_w, step_w, out_w = (
        lax.all_gather(proj_gate, "dp", axis=0, tiled=True),
        lax.all_gather(proj_value, "dp", axis=0, tiled=True),
        lax.all_gather(proj_state, "dp", axis=0, tiled=True),
        lax.all_gather(proj_step, "dp", axis=0, tiled=True),
        lax.all_gather(proj_out, "dp", axis=1, tiled=True),
    )
    resid_wide = resid_full.astype(jnp.float32)
    inv_rms = lax.rsqrt(jnp.mean(resid_wide * resid_wide, axis=-1, keepdims=True) + epsilon)
    unit_rows = resid_wide * inv_rms
    gain_wide = gain_row.astype(jnp.float32)
    normed_in = (unit_rows * gain_wide).astype(jnp.bfloat16)
    gate_raw = product(normed_in, gate_w)
    value_raw = product(normed_in, value_w)
    state_raw = product(normed_in, state_w)
    step_raw = product(normed_in, step_w)
    seq_count = resid_in.shape[0] // SEQ

    def conv_act(raw, kernel, kernel_bias):
        framed = raw.reshape(seq_count, SEQ, raw.shape[1])
        convolved = jax.vmap(causal_conv, (0, None, None))(framed, kernel, kernel_bias)
        return jax.nn.silu(convolved).reshape(raw.shape)

    value_act, value_pull = jax.vjp(conv_act, value_raw, conv_value, value_bias)
    values = value_act.astype(jnp.bfloat16)
    state_act, state_pull = jax.vjp(conv_act, state_raw, conv_state, state_bias)
    maps = lax.all_gather(state_act.astype(jnp.bfloat16), "tp", axis=1, tiled=True)
    head_count = step_raw.shape[1]
    state_dim = maps.shape[1] // 2

    def mixer(values_in, maps_in, step_in, bias_in, log_in, skip_in):
        step_size = jax.nn.softplus(step_in + bias_in)
        scan_one = partial(ssd, group_len=GROUP)
        mixed_out = jax.vmap(scan_one, (0, 0, 0, 0, None, None))(
            values_in.reshape(seq_count, SEQ, head_count, HEADDIM),
            step_size.reshape(seq_count, SEQ, head_count),
            maps_in[:, :state_dim].reshape(seq_count, SEQ, state_dim),
            maps_in[:, state_dim:].reshape(seq_count, SEQ, state_dim),
            -jnp.exp(log_in),
            skip_in,
        )
        return mixed_out.reshape(values_in.shape)

    mixed, mixer_pull = jax.vjp(
        mixer,
        values.astype(jnp.float32),
        maps.astype(jnp.float32),
        step_raw,
        step_bias,
        decay_log,
        skip_gain,
    )
    gated, gate_pull = jax.vjp(gating, mixed, gate_raw)
    squares = lax.psum(jnp.sum(gated * gated, axis=-1), "tp")
    gate_scale = lax.rsqrt(squares / INNER + epsilon)[:, None]
    scaled = gated * gate_scale
    normed_out = (scaled * gate_gain).astype(jnp.bfloat16)
    out_terms = product(normed_out, out_w)
    out_mine = lax.psum_scatter(out_terms, "tp", scatter_dimension=1, tiled=True)
    block_out = (resid_in.astype(jnp.float32) + out_mine).astype(jnp.bfloat16)
    normed_grad = product_right(cot_full, out_w)
    out_grad = product_left(normed_out, cot_full)
    gate_gain_grad = jnp.sum(normed_grad * scaled, axis=0)
    weighted = normed_grad * gate_gain
    crossed = lax.psum(jnp.sum(weighted * gated, axis=-1), "tp")
    cubed = gate_scale * gate_scale * gate_scale
    gated_grad = weighted * gate_scale - gated * cubed * (crossed[:, None] / INNER)
    mixed_grad, gate_raw_grad = gate_pull(gated_grad)
    values_grad, maps_grad, step_grad, step_bias_grad, decay_grad, skip_grad = mixer_pull(
        mixed_grad
    )
    maps_mine = lax.psum_scatter(maps_grad, "tp", scatter_dimension=1, tiled=True)
    value_raw_grad, conv_value_grad, value_bias_grad = value_pull(values_grad)
    state_raw_grad, conv_state_grad, state_bias_grad = state_pull(maps_mine)
    gate_low = gate_raw_grad.astype(jnp.bfloat16)
    value_low = value_raw_grad.astype(jnp.bfloat16)
    state_low = state_raw_grad.astype(jnp.bfloat16)
    step_low = step_grad.astype(jnp.bfloat16)
    gate_w_grad = product_left(normed_in, gate_low)
    value_w_grad = product_left(normed_in, value_low)
    state_w_grad = product_left(normed_in, state_low)
    step_w_grad = product_left(normed_in, step_low)
    input_terms = (
        product_right(gate_low, gate_w)
        + product_right(value_low, value_w)
        + product_right(state_low, state_w)
        + product_right(step_low, step_w)
    )
    width_mine = resid_in.shape[1]
    start = lax.axis_index("tp") * width_mine
    unit_mine = lax.dynamic_slice_in_dim(unit_rows, start, width_mine, 1)
    resid_mine = resid_in.astype(jnp.float32)
    gain_mine = norm_gain.astype(jnp.float32)
    input_whole = lax.psum(input_terms, "tp")
    crossed_rows = jnp.sum(input_whole * gain_wide * resid_wide, axis=-1)
    input_mine = lax.dynamic_slice_in_dim(input_whole, start, width_mine, 1)
    pulled = input_mine * gain_mine
    rms_cubed = inv_rms * inv_rms * inv_rms
    grad_in = (
        cotangent.astype(jnp.float32)
        + pulled * inv_rms
        - resid_mine * rms_cubed * (crossed_rows[:, None] / D)
    ).astype(jnp.bfloat16)
    gain_grad = jnp.sum(input_mine * unit_mine, axis=0)
    large_sums = (
        lax.psum_scatter(gate_w_grad, "dp", scatter_dimension=0, tiled=True),
        lax.psum_scatter(value_w_grad, "dp", scatter_dimension=0, tiled=True),
        lax.psum_scatter(state_w_grad, "dp", scatter_dimension=0, tiled=True),
        lax.psum_scatter(step_w_grad, "dp", scatter_dimension=0, tiled=True),
        lax.psum_scatter(out_grad, "dp", scatter_dimension=1, tiled=True),
    )
    small_sums = lax.psum(
        (
            gain_grad,
            conv_value_grad,
            value_bias_grad,
            conv_state_grad,
            state_bias_grad,
            step_bias_grad,
            decay_grad,
            skip_grad,
            gate_gain_grad,
        ),
        "dp",
    )
    return (
        block_out,
        grad_in,
        small_sums[0],
        large_sums[0],
        large_sums[1],
        large_sums[2],
        large_sums[3],
        small_sums[1],
        small_sums[2],
        small_sums[3],
        small_sums[4],
        small_sums[5],
        small_sums[6],
        small_sums[7],
        small_sums[8],
        large_sums[4],
    )


CHUNK = 128
QUAD = 8
WIDE = QUAD * HEADDIM
F32 = jnp.float32
BF16 = jnp.bfloat16


def nt(left, right):
    return lax.dot_general(left, right, (((1,), (1,)), ((), ())), preferred_element_type=F32)


def nn(left, right):
    return jnp.dot(left, right, preferred_element_type=F32)


def parts(v):
    high = v.astype(BF16)
    return high, (v - high.astype(F32)).astype(BF16)


def twice(v, axis=1):
    return jnp.concatenate([v, v], axis=axis)


def stacked(pair, axis=0):
    return jnp.concatenate(pair, axis=axis)


def nt_parts(left, right):
    return nt(left[0], right[0]) + nt(left[0], right[1]) + nt(left[1], right[0])


def pair_columns(ref, pair, lane_low):
    first = jnp.broadcast_to(ref[0, :, 2 * pair : 2 * pair + 1], (CHUNK, 128))
    second = jnp.broadcast_to(ref[0, :, 2 * pair + 1 : 2 * pair + 2], (CHUNK, 128))
    return first, second, jnp.where(lane_low, first, second)


def two_heads(block, lane_low):
    zero = jnp.zeros_like(block)
    return jnp.concatenate([jnp.where(lane_low, block, zero), jnp.where(lane_low, zero, block)], axis=0)


def shifts(before, raw):
    longer = jnp.concatenate([before, raw], axis=0)
    return [longer[5 + tap : 5 + tap + CHUNK] for tap in range(4)]


def convolved(shifted, taps_ref, bias_ref):
    total = bias_ref[...] + taps_ref[0:1, :] * shifted[0]
    for tap in range(1, 4):
        total = total + taps_ref[tap : tap + 1, :] * shifted[tap]
    return total


def scan_forward(per_seq, raw_ref, taps_ref, bias_ref, b_ref, c_ref, bt_ref, acol_ref, dtcol_ref, arow_ref, skip_ref, x_ref, y_ref, st_ref, state, scores, tails):
    step, quad = pl.program_id(0), pl.program_id(1)
    row = lax.broadcasted_iota(jnp.int32, (CHUNK, CHUNK), 0)
    col = lax.broadcasted_iota(jnp.int32, (CHUNK, CHUNK), 1)
    lane_low = col < HEADDIM

    @pl.when(lax.rem(step, per_seq) == 0)
    def _():
        state[quad] = jnp.zeros((CHUNK, WIDE), F32)
        tails[quad] = jnp.zeros((8, WIDE), F32)

    @pl.when(quad == 0)
    def _():
        scores[...] = jnp.where(row >= col, nt(c_ref[...], b_ref[...]), 0.0)

    raw = raw_ref[...]
    pre = convolved(shifts(tails[quad], raw), taps_ref, bias_ref)
    tails[quad] = raw[CHUNK - 8 :]
    x_ref[...] = (pre * jax.nn.sigmoid(pre)).astype(BF16)
    entering = state[quad]
    st_ref[0] = entering
    across = nn(twice(c_ref[...]), stacked(parts(entering)))
    within = scores[...]
    ends, rights = [], []
    for pair in range(QUAD // 2):
        lanes = slice(128 * pair, 128 * pair + 128)
        x = x_ref[:, lanes].astype(F32)
        a1, a2, asel = pair_columns(acol_ref, pair, lane_low)
        _, _, dsel = pair_columns(dtcol_ref, pair, lane_low)
        u = x * dsel
        m1 = within * jnp.exp(jnp.minimum(a1 - arow_ref[0, 2 * pair : 2 * pair + 1, :], 0.0))
        m2 = within * jnp.exp(jnp.minimum(a2 - arow_ref[0, 2 * pair + 1 : 2 * pair + 2, :], 0.0))
        both = jnp.concatenate([m1.astype(BF16), m2.astype(BF16)], axis=1)
        y = nn(both, two_heads(u.astype(BF16), lane_low))
        y_ref[:, lanes] = y + jnp.exp(asel) * across[:, lanes] + skip_ref[:, lanes] * x
        last = asel[CHUNK - 1 : CHUNK, :]
        rights.append(jnp.exp(last - asel) * u)
        ends.append(jnp.exp(last))
    added = nn(twice(bt_ref[...]), stacked(parts(jnp.concatenate(rights, axis=1))))
    state[quad] = jnp.concatenate(ends, axis=1) * entering + added


def scan_backward(per_seq, quads, x_ref, raw_ref, before_ref, taps_ref, bias_ref, dy_ref, b_ref, c_ref, ct_ref, acol_ref, dtcol_ref, arow_ref, skip_ref, st_ref, pick_ref,
                  dx_ref, db_ref, dc_ref, small_ref, dskip_ref, dconv_ref, grads, scores, scores_t, dscores, heads):
    step, quad = pl.program_id(0), pl.program_id(1)
    row = lax.broadcasted_iota(jnp.int32, (CHUNK, CHUNK), 0)
    col = lax.broadcasted_iota(jnp.int32, (CHUNK, CHUNK), 1)
    lane_low = col < HEADDIM

    @pl.when(lax.rem(step, per_seq) == 0)
    def _():
        grads[quad] = jnp.zeros((CHUNK, WIDE), F32)
        heads[quad] = jnp.zeros((8, WIDE), F32)

    @pl.when(quad == 0)
    def _():
        scores[...] = jnp.where(row >= col, nt(c_ref[...], b_ref[...]), 0.0)
        scores_t[...] = jnp.where(row <= col, nt(b_ref[...], c_ref[...]), 0.0)
        dscores[...] = jnp.zeros_like(dscores)
        db_ref[...] = jnp.zeros_like(db_ref)
        dc_ref[...] = jnp.zeros_like(dc_ref)

    leaving = grads[quad]
    leaving_parts = parts(leaving)
    entering = st_ref[0]
    entering_parts = parts(entering)
    across = nn(twice(c_ref[...]), stacked(entering_parts))
    from_state = nn(twice(b_ref[...]), stacked(leaving_parts))
    kept = jnp.sum(leaving * entering, axis=0, keepdims=True)
    within, within_t = scores[...], scores_t[...]
    dwithin = jnp.zeros((CHUNK, CHUNK), F32)
    ends, rights, reads, his, los, steps, dxs = [], [], [], [], [], [], []
    for pair in range(QUAD // 2):
        lanes = slice(128 * pair, 128 * pair + 128)
        x = x_ref[:, lanes].astype(F32)
        dy = dy_ref[:, lanes]
        dy_low = dy.astype(BF16)
        dy_back = dy_low.astype(F32)
        a1, a2, asel = pair_columns(acol_ref, pair, lane_low)
        _, _, dsel = pair_columns(dtcol_ref, pair, lane_low)
        r1 = arow_ref[0, 2 * pair : 2 * pair + 1, :]
        r2 = arow_ref[0, 2 * pair + 1 : 2 * pair + 2, :]
        d1, d2 = a1 - r1, a2 - r2
        l1, l2 = jnp.exp(jnp.minimum(d1, 0.0)), jnp.exp(jnp.minimum(d2, 0.0))
        t1, t2 = jnp.exp(jnp.minimum(-d1, 0.0)), jnp.exp(jnp.minimum(-d2, 0.0))
        u = x * dsel
        u_low = u.astype(BF16)
        u_back = u_low.astype(F32)
        dy_two = two_heads(dy_low, lane_low)
        both = jnp.concatenate([(within * l1).astype(BF16), (within * l2).astype(BF16)], axis=1)
        both_t = jnp.concatenate([(within_t * t1).astype(BF16), (within_t * t2).astype(BF16)], axis=1)
        y = nn(both, two_heads(u_low, lane_low))
        du = nn(both_t, dy_two)
        w = nt(stacked((dy_two, two_heads((dy - dy_back).astype(BF16), lane_low)), 1), twice(u_low))
        dwithin = dwithin + l1 * w[:CHUNK] + l2 * w[CHUNK:]
        last = asel[CHUNK - 1 : CHUNK, :]
        last_decay = jnp.exp(last)
        into = jnp.exp(asel)
        out_of = jnp.exp(last - asel)
        du_state = out_of * from_state[:, lanes]
        du_all = du + du_state
        dxs.append(dsel * du_all + skip_ref[:, lanes] * dy)
        passed = u * du_state
        final = jnp.sum(passed, axis=0, keepdims=True) + last_decay * kept[:, lanes]
        read = dy * into
        da = dy_back * y + read * across[:, lanes] - u_back * du - passed
        da = da + jnp.where(row == CHUNK - 1, final, 0.0)
        da_hi = da.astype(BF16)
        his.append(da_hi)
        los.append((da - da_hi.astype(F32)).astype(BF16))
        steps.append((x * du_all).astype(BF16))
        reads.append(read)
        rights.append(out_of * u)
        ends.append(last_decay)
        dskip_ref[0, :, lanes] = jnp.sum((dy * x).reshape(CHUNK // 8, 8, 128), axis=0)
    before = jnp.where(lax.rem(step + 1, per_seq) == 0, 0.0, before_ref[...])
    shifted = shifts(before, raw_ref[...])
    pre = convolved(shifted, taps_ref, bias_ref)
    sig = jax.nn.sigmoid(pre)
    dpre = jnp.concatenate(dxs, axis=1) * (sig * (1.0 + pre * (1.0 - sig)))
    longer = jnp.concatenate([dpre, heads[quad]], axis=0)
    heads[quad] = dpre[:8]
    draw = taps_ref[3:4, :] * dpre
    for tap in range(3):
        draw = draw + taps_ref[tap : tap + 1, :] * longer[3 - tap : 3 - tap + CHUNK]
    dx_ref[...] = draw.astype(BF16)
    for tap in range(4):
        dconv_ref[0, 8 * tap : 8 * tap + 8, :] = jnp.sum((dpre * shifted[tap]).reshape(CHUNK // 8, 8, WIDE), axis=0)
    dconv_ref[0, 32:40, :] = jnp.sum(dpre.reshape(CHUNK // 8, 8, WIDE), axis=0)
    read = parts(jnp.concatenate(reads, axis=1))
    right = parts(jnp.concatenate(rights, axis=1))
    dscores[...] += dwithin
    dc_ref[...] += nt_parts(read, entering_parts)
    db_ref[...] += nt_parts(right, leaving_parts)
    grads[quad] = jnp.concatenate(ends, axis=1) * leaving + nn(twice(ct_ref[...]), stacked(read))
    small_ref[0] = nn(jnp.concatenate(his + los + steps, axis=1), pick_ref[...])

    @pl.when(quad == quads - 1)
    def _():
        total = jnp.where(row >= col, dscores[...], 0.0)
        dc_ref[...] += nn(stacked(parts(total), 1), twice(b_ref[...], 0))
        db_ref[...] += nn(stacked(parts(total.T), 1), twice(c_ref[...], 0))


def scan_inputs(maps, log_decay, step_size):
    tokens, heads = step_size.shape
    quads = heads // QUAD
    columns = lambda v: v.reshape(tokens, quads, QUAD).transpose(1, 0, 2)
    rows = log_decay.T.reshape(quads, QUAD, tokens)
    half = maps.shape[1] // 2
    return maps[:, :half], maps[:, half:], columns(log_decay), columns(step_size), rows


def run_forward(raw, taps, bias, maps, log_decay, step_size, skip_lanes):
    tokens, inner = raw.shape
    quads, chunks = inner // WIDE, tokens // CHUNK
    enter, read, acol, dtcol, arow = scan_inputs(maps, log_decay, step_size)
    lane = lambda height: pl.BlockSpec((height, WIDE), lambda i, q: (0, q))
    tall = lambda: pl.BlockSpec((CHUNK, WIDE), lambda i, q: (i, q))
    thin = lambda: pl.BlockSpec((CHUNK, CHUNK), lambda i, q: (i, 0))
    cols = lambda: pl.BlockSpec((1, CHUNK, QUAD), lambda i, q: (q, i, 0))
    return pl.pallas_call(
        partial(scan_forward, SEQ // CHUNK),
        grid=(chunks, quads),
        in_specs=[tall(), lane(4), lane(1), thin(), thin(), pl.BlockSpec((CHUNK, CHUNK), lambda i, q: (0, i)), cols(), cols(),
                  pl.BlockSpec((1, QUAD, CHUNK), lambda i, q: (q, 0, i)), pl.BlockSpec((1, WIDE), lambda i, q: (0, q))],
        out_specs=[tall(), tall(), pl.BlockSpec((1, CHUNK, WIDE), lambda i, q: (i, 0, q))],
        out_shape=[jax.ShapeDtypeStruct((tokens, inner), BF16), jax.ShapeDtypeStruct((tokens, inner), F32), jax.ShapeDtypeStruct((chunks, CHUNK, inner), F32)],
        scratch_shapes=[pltpu.VMEM((quads, CHUNK, WIDE), F32), pltpu.VMEM((CHUNK, CHUNK), F32), pltpu.VMEM((quads, 8, WIDE), F32)],
        compiler_params=pltpu.CompilerParams(vmem_limit_bytes=32 * 2**20),
        cost_estimate=pl.CostEstimate(flops=tokens * inner * 1024, bytes_accessed=tokens * inner * 10, transcendentals=tokens * inner * 4),
        name="scan_forward",
    )(raw, taps, bias[None, :], enter, read, enter.T, acol, dtcol, arow, skip_lanes)


def run_backward(values, raw, taps, bias, dmixed, maps, log_decay, step_size, skip_lanes, states):
    tokens, inner = values.shape
    quads, chunks = inner // WIDE, tokens // CHUNK
    enter, read, acol, dtcol, arow = scan_inputs(maps, log_decay, step_size)
    lane_head = jnp.arange(WIDE)[:, None] // HEADDIM
    pick = lambda base: (lane_head + base == jnp.arange(128)[None, :]).astype(BF16)
    picks = jnp.concatenate([pick(0), pick(0), pick(QUAD)], axis=0)
    end = chunks - 1
    tall = lambda: pl.BlockSpec((CHUNK, WIDE), lambda i, q: (end - i, q))
    thin = lambda: pl.BlockSpec((CHUNK, CHUNK), lambda i, q: (end - i, 0))
    cols = lambda: pl.BlockSpec((1, CHUNK, QUAD), lambda i, q: (q, end - i, 0))
    lane = lambda height: pl.BlockSpec((height, WIDE), lambda i, q: (0, q))
    before = pl.BlockSpec((8, WIDE), lambda i, q: (jnp.maximum((end - i) * (CHUNK // 8) - 1, 0), q))
    dx, db, dc, small, dskip, dconv = pl.pallas_call(
        partial(scan_backward, SEQ // CHUNK, quads),
        grid=(chunks, quads),
        in_specs=[tall(), tall(), before, lane(4), lane(1), tall(), thin(), thin(), pl.BlockSpec((CHUNK, CHUNK), lambda i, q: (0, end - i)), cols(), cols(),
                  pl.BlockSpec((1, QUAD, CHUNK), lambda i, q: (q, 0, end - i)), pl.BlockSpec((1, WIDE), lambda i, q: (0, q)),
                  pl.BlockSpec((1, CHUNK, WIDE), lambda i, q: (end - i, 0, q)), pl.BlockSpec((3 * WIDE, 128), lambda i, q: (0, 0))],
        out_specs=[tall(), thin(), thin(), pl.BlockSpec((1, CHUNK, 128), lambda i, q: (q, end - i, 0)),
                   pl.BlockSpec((1, 8, WIDE), lambda i, q: (end - i, 0, q)),
                   pl.BlockSpec((1, 40, WIDE), lambda i, q: (end - i, 0, q))],
        out_shape=[jax.ShapeDtypeStruct((tokens, inner), BF16), jax.ShapeDtypeStruct((tokens, CHUNK), F32),
                   jax.ShapeDtypeStruct((tokens, CHUNK), F32), jax.ShapeDtypeStruct((quads, tokens, 128), F32),
                   jax.ShapeDtypeStruct((chunks, 8, inner), F32), jax.ShapeDtypeStruct((chunks, 40, inner), F32)],
        scratch_shapes=[pltpu.VMEM((quads, CHUNK, WIDE), F32)] + [pltpu.VMEM((CHUNK, CHUNK), F32)] * 3 + [pltpu.VMEM((quads, 8, WIDE), F32)],
        compiler_params=pltpu.CompilerParams(vmem_limit_bytes=32 * 2**20),
        cost_estimate=pl.CostEstimate(flops=tokens * inner * 2560, bytes_accessed=tokens * inner * 12, transcendentals=tokens * inner * 8),
        name="scan_backward",
    )(values, raw, raw, taps, bias[None, :], dmixed, enter, read, read.T, acol, dtcol, arow, skip_lanes, states, picks)
    per_head = lambda part: part.transpose(1, 0, 2).reshape(tokens, quads * QUAD)
    dlog = per_head(small[:, :, :QUAD])
    dstep = per_head(small[:, :, QUAD : 2 * QUAD])
    dskip = jnp.sum(dskip.reshape(chunks * 8, inner // HEADDIM, HEADDIM), axis=(0, 2))
    dconv = jnp.sum(dconv.reshape(chunks, 5, 8, inner), axis=(0, 2))
    return dx, jnp.concatenate([db, dc], axis=1), dlog, dstep, dskip, dconv


def chunk_sums(v, lower):
    tokens, heads = v.shape
    framed = v.reshape(tokens // CHUNK, CHUNK, heads)
    ones = jnp.tril(jnp.ones((CHUNK, CHUNK), F32))
    ones = ones if lower else ones.T
    return jnp.einsum("ts,csh->cth", ones, framed, precision=lax.Precision.HIGHEST).reshape(tokens, heads)


def to_sequences(block):
    me = lax.axis_index("tp")
    rows = block.shape[0] // 2
    mine = lax.dynamic_slice_in_dim(block, me * rows, rows, 0)
    other = lax.dynamic_slice_in_dim(block, (1 - me) * rows, rows, 0)
    came = lax.ppermute(other, "tp", [(0, 1), (1, 0)])
    first = me == 0
    return jnp.concatenate([jnp.where(first, mine, came), jnp.where(first, came, mine)], axis=1)


def to_features(block):
    me = lax.axis_index("tp")
    cols = block.shape[1] // 2
    mine = lax.dynamic_slice_in_dim(block, me * cols, cols, 1)
    other = lax.dynamic_slice_in_dim(block, (1 - me) * cols, cols, 1)
    came = lax.ppermute(other, "tp", [(0, 1), (1, 0)])
    first = me == 0
    return jnp.concatenate([jnp.where(first, mine, came), jnp.where(first, came, mine)], axis=0)


def gather_columns(shards, wide):
    widths = [shard.shape[1] for shard in shards]
    pieces, at = [], 0
    for width in widths:
        pieces += [wide[part, :, at : at + width] for part in range(wide.shape[0])]
        at += width
    return lax.all_gather(jnp.concatenate(pieces, axis=1), "dp", axis=0, tiled=True)


def sum_half(whole, axis):
    me = lax.axis_index("tp")
    size = whole.shape[axis] // 2
    mine = lax.dynamic_slice_in_dim(whole, me * size, size, axis)
    other = lax.dynamic_slice_in_dim(whole, (1 - me) * size, size, axis).astype(BF16)
    return mine + lax.ppermute(other, "tp", [(0, 1), (1, 0)]).astype(F32)


def sum_rows(halves):
    return lax.psum_scatter(halves, "dp", scatter_dimension=0, tiled=True)


def by_sequences(
    tp,
    resid_in,
    norm_gain,
    proj_gate,
    proj_value,
    proj_state,
    proj_step,
    conv_value,
    value_bias,
    conv_state,
    state_bias,
    step_bias,
    decay_log,
    skip_gain,
    gate_gain,
    proj_out,
    cotangent,
):
    small_in = [norm_gain.astype(F32), conv_value, value_bias, conv_state, state_bias, step_bias, decay_log, skip_gain, gate_gain]
    packed = lax.all_gather(jnp.concatenate([v.reshape(-1) for v in small_in]), "tp", axis=0)
    fulls, at = [], 0
    for v in small_in:
        piece = packed[:, at : at + v.size].reshape((tp,) + v.shape)
        at += v.size
        fulls.append(piece.reshape(-1) if v.ndim == 1 else piece.transpose(1, 0, 2).reshape(v.shape[0], -1))
    low_parts = [proj_value, proj_state, proj_step]
    low_wide = lax.all_gather(jnp.concatenate(low_parts, axis=1), "tp", axis=0)
    gate_wide = lax.all_gather(proj_gate, "tp", axis=0)
    out_rows = lax.all_gather(proj_out, "tp", axis=0, tiled=True)
    resid_in, cotangent, low_wide, gate_wide, out_rows, fulls = lax.optimization_barrier(
        (resid_in, cotangent, low_wide, gate_wide, out_rows, fulls)
    )
    gain, conv_v, bias_v, conv_s, bias_s, bias_step, log_rate, skip, gain_out = fulls
    resid = to_sequences(resid_in).astype(F32)
    low_w = gather_columns(low_parts, low_wide)
    gate_w = gather_columns([proj_gate], gate_wide)
    out_w = lax.all_gather(out_rows, "dp", axis=1, tiled=True)
    cot_low = to_sequences(cotangent)

    tokens = resid.shape[0]
    seqs = tokens // SEQ
    inner = gate_w.shape[1]
    states = conv_s.shape[1]
    value_w, rest_w = low_w[:, :inner], low_w[:, inner:]

    inv_rms = lax.rsqrt(jnp.mean(resid * resid, axis=-1, keepdims=True) + epsilon)
    unit_rows = resid * inv_rms
    normed_in = (unit_rows * gain).astype(BF16)
    value_raw = product(normed_in, value_w)
    rest_raw = product(normed_in, rest_w)
    state_raw, step_raw = rest_raw[:, :states], rest_raw[:, states:]

    def conv_act(raw, kernel, kernel_bias):
        framed = raw.reshape(seqs, SEQ, raw.shape[1])
        convolved = jax.vmap(causal_conv, (0, None, None))(framed, kernel, kernel_bias)
        return jax.nn.silu(convolved).reshape(raw.shape)

    state_act, state_pull = jax.vjp(conv_act, state_raw, conv_s, bias_s)
    maps = state_act.astype(BF16)
    step_size, step_pull = jax.vjp(lambda v: jax.nn.softplus(v + bias_step), step_raw)
    rate = -jnp.exp(log_rate)
    log_decay = chunk_sums(step_size * rate, True)
    skip_lanes = jnp.repeat(skip, HEADDIM)[None, :]
    values, mixed, entering = run_forward(value_raw, conv_v, bias_v, maps, log_decay, step_size, skip_lanes)

    gate_raw = product(normed_in, gate_w)
    gated, gate_pull = jax.vjp(gating, mixed, gate_raw)
    squares = jnp.sum(gated * gated, axis=-1, keepdims=True)
    gate_scale = lax.rsqrt(squares / inner + epsilon)
    scaled = gated * gate_scale
    normed_out = (scaled * gain_out).astype(BF16)
    block_out = to_features((resid + product(normed_out, out_w)).astype(BF16))
    normed_grad = product_right(cot_low, out_w)
    out_grad = product_left(cot_low, normed_out)
    gate_gain_grad = jnp.sum(normed_grad * scaled, axis=0)
    weighted = normed_grad * gain_out
    crossed = jnp.sum(weighted * gated, axis=-1, keepdims=True)
    cubed = gate_scale * gate_scale * gate_scale
    gated_grad = weighted * gate_scale - gated * cubed * (crossed / inner)
    mixed_grad, gate_raw_grad = gate_pull(gated_grad)
    gate_low = gate_raw_grad.astype(BF16)
    gate_w_grad = product_left(normed_in, gate_low)
    early_half = jnp.concatenate([sum_half(gate_w_grad, 1), sum_half(out_grad, 1)], axis=1)
    mixed_grad, early_half = lax.optimization_barrier((mixed_grad, early_half))
    early_mine = sum_rows(early_half)

    value_low, maps_grad, dlog, dstep, skip_grad, conv_grads = run_backward(
        values, value_raw, conv_v, bias_v, mixed_grad, maps, log_decay, step_size, skip_lanes, entering
    )
    value_low, early_mine = lax.optimization_barrier((value_low, early_mine))
    gate_mine, out_mine = early_mine[:, : inner // 2], early_mine[:, inner // 2 :].T
    summed = chunk_sums(dlog, False)
    decay_grad = rate * jnp.sum(summed * step_size, axis=0)
    (step_grad,) = step_pull(dstep + summed * rate)
    step_bias_grad = jnp.sum(step_grad, axis=0)
    conv_value_grad, value_bias_grad = conv_grads[:4], conv_grads[4]
    state_raw_grad, conv_state_grad, state_bias_grad = state_pull(maps_grad)
    rest_low = jnp.concatenate([state_raw_grad.astype(BF16), step_grad.astype(BF16)], axis=1)
    value_w_grad = product_left(normed_in, value_low)
    rest_w_grad = product_left(normed_in, rest_low)
    low_half = [sum_half(v, 1) for v in (value_w_grad, rest_w_grad[:, :states], rest_w_grad[:, states:])]
    low_mine = sum_rows(jnp.concatenate(low_half, axis=1))
    value_mine = low_mine[:, : inner // 2]
    state_mine = low_mine[:, inner // 2 : (inner + states) // 2]
    step_mine = low_mine[:, (inner + states) // 2 :]
    input_grad = (
        product_right(gate_low, gate_w) + product_right(value_low, value_w) + product_right(rest_low, rest_w)
    )
    gain_grad = jnp.sum(input_grad * unit_rows, axis=0)
    pulled = input_grad * gain
    crossed_rows = jnp.sum(pulled * resid, axis=-1, keepdims=True)
    rms_cubed = inv_rms * inv_rms * inv_rms
    grad_in = (
        cot_low.astype(F32) + pulled * inv_rms - resid * rms_cubed * (crossed_rows / resid.shape[1])
    ).astype(BF16)
    grad_in = to_features(grad_in)

    small_out = [gain_grad, conv_value_grad, value_bias_grad, conv_state_grad, state_bias_grad, step_bias_grad, decay_grad, skip_grad, gate_gain_grad]
    split = [
        v.reshape(tp, -1) if v.ndim == 1 else v.reshape(v.shape[0], tp, -1).transpose(1, 0, 2).reshape(tp, -1)
        for v in small_out
    ]
    sums = lax.psum(jnp.concatenate(split, axis=1), ("dp", "tp"))
    mine = lax.dynamic_slice_in_dim(sums, lax.axis_index("tp"), 1, 0)[0]
    smalls, at = [], 0
    for v in small_in:
        smalls.append(mine[at : at + v.size].reshape(v.shape))
        at += v.size
    return (
        block_out,
        grad_in,
        smalls[0],
        gate_mine,
        value_mine,
        state_mine,
        step_mine,
        *smalls[1:],
        out_mine,
    )


def solution(mesh):
    tp = mesh.shape["tp"]

    def local(*args):
        seqs = args[0].shape[0] // SEQ
        if seqs % tp == 0 and tp == 2:
            return by_sequences(tp, *args)
        return by_heads(*args)

    return jax.shard_map(
        local,
        mesh=mesh,
        in_specs=(
            P("dp", "tp"),
            P("tp"),
            P("dp", "tp"),
            P("dp", "tp"),
            P("dp", "tp"),
            P("dp", "tp"),
            P(None, "tp"),
            P("tp"),
            P(None, "tp"),
            P("tp"),
            P("tp"),
            P("tp"),
            P("tp"),
            P("tp"),
            P("tp", "dp"),
            P("dp", "tp"),
        ),
        out_specs=(
            P("dp", "tp"),
            P("dp", "tp"),
            P("tp"),
            P("dp", "tp"),
            P("dp", "tp"),
            P("dp", "tp"),
            P("dp", "tp"),
            P(None, "tp"),
            P("tp"),
            P(None, "tp"),
            P("tp"),
            P("tp"),
            P("tp"),
            P("tp"),
            P("tp"),
            P("tp", "dp"),
        ),
        check_vma=False,
    )
```
